32 devices in a mesh: tm: 4 (over y, x), space: 8 (over z, core).
Axes of the slice: x: 2, y: 2, z: 4, core: 2. Of those that a mesh axis runs over, the one named last changes fastest.
Arguments:
- q_start: float32 [5, 32, 64, 128], P(None, 'space'), may hold values from -3.6 to 3.6
- guess: float32 [4, 5, 32, 64, 128], P('tm', None, 'space'), may hold values from -3.6 to 3.6
Outputs:
- corrected: float32 [4, 5, 32, 64, 128], P('tm', None, 'space')
- residual: float32 [4, 5, 32, 64, 128], P('tm', None, 'space')
The draws below stay inside these ranges and needn't reach their ends.
All inputs are finite; a program needn't handle non-finite values.
Results may differ from the reference program's by a relative error of at most 0.00011.
Values sent between devices are 32-bit elements; how exact they have to be, the bound alone decides.
A program may use at most 64 MiB of HBM per device.

```python
import math
import jax
import jax.numpy as jnp
from jax import lax

BX = 4
NY = 64
NZ = 128
COMP = 5
STEPS_SLAB = 2
SWEEPS = 2
BLK = 4
NX = 32
SLABS = 4


def field_parts(key, slabs):
    keys = jax.random.split(key, 11)
    shape = (slabs, COMP, NX, NY, NZ)
    row_index = lax.broadcasted_iota(jnp.int32, shape, 2)
    col_index = lax.broadcasted_iota(jnp.int32, shape, 3)
    depth_index = lax.broadcasted_iota(jnp.int32, shape, 4)
    x_coord = (row_index.astype(jnp.float32) + 0.5) / NX
    y_coord = col_index.astype(jnp.float32) / NY
    z_coord = depth_index.astype(jnp.float32) / NZ
    modes = 3
    mode_shape = (modes, slabs, COMP, 1, 1, 1)
    wave_x = jax.random.randint(keys[0], mode_shape, 0, 3).astype(jnp.float32)
    wave_y = jax.random.randint(keys[1], mode_shape, 0, 3).astype(jnp.float32)
    wave_z = jax.random.randint(keys[2], mode_shape, 0, 3).astype(jnp.float32)
    phases = jax.random.uniform(keys[3], mode_shape, jnp.float32, 0.0, 2.0 * math.pi)
    weights = jax.random.uniform(keys[4], mode_shape, jnp.float32, 0.3, 0.5)
    smooth = jnp.zeros(shape, jnp.float32)
    for mode in range(modes):
        angle = math.pi * wave_x[mode] * x_coord + 2.0 * math.pi * (wave_y[mode] * y_coord + wave_z[mode] * z_coord) + phases[mode]
        smooth = smooth + weights[mode] * jnp.cos(angle)
    rough_flat = jax.random.uniform(keys[5], shape, jnp.float32, -0.9, 0.9)
    rough_normal = 0.5 * jax.random.truncated_normal(keys[6], -3.0, 3.0, shape, jnp.float32)
    level_signed = jax.random.uniform(keys[7], (slabs, COMP, 1, 1, 1), jnp.float32, -0.6, 0.6)
    level_plus = jax.random.uniform(keys[8], (slabs, COMP, 1, 1, 1), jnp.float32, 0.2, 1.4)
    block_shape = (slabs, COMP, NX // BX, 1, 1)
    block_offset = jax.random.uniform(keys[9], block_shape, jnp.float32, -0.8, 0.8)
    block_offset = jnp.repeat(block_offset, BX, axis=2)
    block_amplitude = jax.random.uniform(keys[10], block_shape, jnp.float32, 0.3, 1.6)
    block_amplitude = jnp.repeat(block_amplitude, BX, axis=2)
    return (smooth, rough_flat, rough_normal, level_signed, level_plus, block_offset, block_amplitude)


def compose(parts):
    smooth, rough_flat, rough_normal, level_signed, level_plus, block_offset, block_amplitude = parts
    value = level_signed + block_offset + smooth + block_amplitude * rough_normal
    return jnp.clip(value, -3.6, 3.6)


def draw_q_start(key, part):
    return compose(field_parts(jax.random.fold_in(key, 11), 1))[0]


def draw_guess(key, part):
    return compose(field_parts(jax.random.fold_in(key, 23), SLABS))


def setup_inputs(seed: int = 0) -> dict:
    seeds = jax.random.split(jax.random.key(seed), 3)
    return {
        "q_start": draw_q_start(jax.random.fold_in(seeds[2], 71), 0),
        "guess": draw_guess(jax.random.fold_in(seeds[2], 71), 0),
    }


time_step = 0.1
cross = 8.0
axial = 2.0
linear_rate = 0.1
quadratic_rate = 0.5
cubic_rate = 1.0


def bulk_terms(field):
    first, second, third, fourth, fifth = field[0], field[1], field[2], field[3], field[4]
    sixth = -first - fourth
    s_aa = first * first + second * second + third * third
    s_ab = first * second + second * fourth + third * fifth
    s_ac = first * third + second * fifth + third * sixth
    s_bb = second * second + fourth * fourth + fifth * fifth
    s_bc = second * third + fourth * fifth + fifth * sixth
    trace = first * first + fourth * fourth + sixth * sixth + 2.0 * (second * second + third * third + fifth * fifth)
    quad = jnp.stack([s_aa - trace / 3.0, s_ab, s_ac, s_bb - trace / 3.0, s_bc])
    source = field + time_step * quadratic_rate * quad
    diagonal = 1.0 + time_step * (linear_rate + cubic_rate * trace) + 2.0 * (2.0 * cross + axial)
    return source, diagonal


def jacobi_sweep(current, source, diagonal):
    padded = jnp.pad(current, ((0, 0), (1, 1), (1, 1), (0, 0)))
    along_x = padded[:, :-2, 1:-1] + padded[:, 2:, 1:-1]
    along_y = padded[:, 1:-1, :-2] + padded[:, 1:-1, 2:]
    along_z = jnp.roll(current, 1, 3) + jnp.roll(current, -1, 3)
    return (source + cross * (along_x + along_y) + axial * along_z) / diagonal[None]


def implicit_step(field):
    source, diagonal = bulk_terms(field)
    current = field
    for sweep in range(SWEEPS):
        current = jacobi_sweep(current, source, diagonal)
    return current


def propagate(field):
    for step in range(STEPS_SLAB):
        field = implicit_step(field)
    return field


def restrict(field):
    total = jnp.sum(field, axis=(1, 2))
    total = total.reshape(COMP, NZ // BLK, BLK).sum(axis=2)
    return total / (NX * NY * BLK)


def reference(q_start, guess):
    starts = jnp.concatenate([q_start[None], guess[:-1]], axis=0)
    relaxed = lax.map(propagate, starts)
    starts_two = jnp.concatenate([q_start[None], relaxed[:-1]], axis=0)
    again = lax.map(propagate, starts_two)
    residual = again - relaxed
    change = again - guess
    coarse = lax.map(restrict, change)
    decay = 1.0 / (1.0 + STEPS_SLAB * time_step * linear_rate)

    def advance(error, term):
        error = decay * error + term
        return error, error

    zero_error = jnp.zeros((COMP, NZ // BLK), jnp.float32)
    last, errors = lax.scan(advance, zero_error, coarse)
    spread = jnp.broadcast_to(errors[:, :, None, None, :, None], (SLABS, COMP, 1, 1, NZ // BLK, BLK))
    spread = spread.reshape(SLABS, COMP, 1, 1, NZ)
    corrected = relaxed + spread
    return corrected, residual
```

```python
import functools

import jax
import jax.numpy as jnp
from jax import lax
from jax.experimental import pallas as pl
from jax.experimental.pallas import tpu as pltpu
from jax.sharding import PartitionSpec as P

STEPS_SLAB = 2
SWEEPS = 2
BLK = 4

time_step = 0.1
cross = 8.0
axial = 2.0
linear_rate = 0.1
quadratic_rate = 0.5
cubic_rate = 1.0

REACH = STEPS_SLAB * SWEEPS
TILE = 8
CHUNKS = 4
MESH = pl.DeviceIdType.MESH


def bulk(field):
    a, b, c, d, e = field
    f = -a - d
    aa, bb, cc, dd, ee, ff = a * a, b * b, c * c, d * d, e * e, f * f
    trace = aa + dd + ff + 2.0 * (bb + cc + ee)
    third = trace * (1.0 / 3.0)
    quad = (
        aa + bb + cc - third,
        a * b + b * d + c * e,
        a * c + b * e + c * f,
        bb + dd + ee - third,
        b * c + d * e + e * f,
    )
    source = [q + (time_step * quadratic_rate) * s for q, s in zip(field, quad)]
    constant = 1.0 + time_step * linear_rate + 2.0 * (2.0 * cross + axial)
    diagonal = constant + (time_step * cubic_rate) * trace
    return source, diagonal


def neighbours(ref, c, r, t, before, now, after, edge=False):
    along_x = before + after
    if edge:
        higher = pltpu.roll(now, TILE - 1, 0)
    else:
        higher = ref[c, r, pl.ds(TILE * t + TILE + 1, TILE), :]
    along_y = ref[c, r, pl.ds(TILE * t + TILE - 1, TILE), :] + higher
    lanes = now.shape[1]
    along_z = pltpu.roll(now, 1, 1) + pltpu.roll(now, lanes - 1, 1)
    return (cross / axial) * (along_x + along_y) + along_z


def tile_rows(ref, r, t):
    at = pl.ds(pl.multiple_of(TILE * t + TILE, TILE), TILE)
    return [ref[c, r, at, :] for c in range(ref.shape[0])]


def first_sweep(ref, out, src, inv, rows, inside, lo, hi, partial):
    comp = ref.shape[0]
    tiles = ref.shape[2] // TILE - 2

    def one(edge, t, carry):
        at = pl.ds(pl.multiple_of(TILE * t + TILE, TILE), TILE)
        before, now = tile_rows(ref, rows[0] - 1, t), tile_rows(ref, rows[0], t)
        for r in rows:
            after = tile_rows(ref, r + 1, t)
            source, diagonal = bulk(now)
            inverse = inside(r) / diagonal
            scaled = axial * inverse
            inv[r, at, :] = scaled
            for c in range(comp):
                part = source[c] * inverse
                src[c, r, at, :] = part
                out[c, r, at, :] = part + scaled * neighbours(
                    ref, c, r, t, before[c], now[c], after[c], edge
                )
            before, now = now, after
        return carry

    if not partial:
        lax.fori_loop(lo, hi, functools.partial(one, False), 0)
        return
    last = hi - 1 + lax.div(hi, tiles)
    lax.fori_loop(lo, last, functools.partial(one, False), 0)
    lax.fori_loop(last, hi, functools.partial(one, True), 0)


def next_sweep(ref, store, src, inv, rows, lo, hi):
    comp = ref.shape[0]

    def one(t, carry):
        at = pl.ds(pl.multiple_of(TILE * t + TILE, TILE), TILE)
        before, now = tile_rows(ref, rows[0] - 1, t), tile_rows(ref, rows[0], t)
        for r in rows:
            after = tile_rows(ref, r + 1, t)
            scaled = inv[r, at, :]
            for c in range(comp):
                store(c, r, t, src[c, r, at, :] + scaled * neighbours(ref, c, r, t, before[c], now[c], after[c]))
            before, now = now, after
        return carry

    lax.fori_loop(lo, hi, one, 0)


def phi(ref, out, w1, w2, src, inv, inside, rows, lo, hi, out_lo, out_hi):
    wide = rows + 2 * REACH

    def keep(c, r, t, value):
        w2[c, r, pl.ds(pl.multiple_of(TILE * t + TILE, TILE), TILE), :] = value

    def last(c, r, t, value):
        out[c, r - REACH, pl.ds(pl.multiple_of(TILE * t, TILE), TILE), :] = value

    first_sweep(ref, w1, src, inv, range(1, wide - 1), inside, lo, hi, True)
    next_sweep(w1, keep, src, inv, range(2, wide - 2), lo, hi)
    first_sweep(w2, w1, src, inv, range(3, wide - 3), inside, lo, hi, False)
    next_sweep(w1, last, src, inv, range(4, wide - 4), out_lo, out_hi)


def kernel(
    n, slabs, q_ref, g_ref, corrected_ref, residual_ref,
    e1, e2, w1, w2, src, inv, x, again, relaxed, guess, result, rest, sums, terms,
    load_sem, h1_send, h1_recv, h2_send, h2_recv, x_send, r_send, f_send, s_recv, r_recv,
    sum_send, sum_recv, term_send, term_recv, out_sem,
):
    p = lax.axis_index("tm")
    s = lax.axis_index("space")
    comp, rows, ny, nz = x.shape
    tiles = ny // TILE
    mid = pl.ds(REACH, rows)
    body = pl.ds(TILE, ny)
    has_left, has_right = s > 0, s < n - 1

    own = e1.at[:, mid, body, :]
    load_guess = pltpu.make_async_copy(g_ref.at[0], guess, load_sem.at[0])
    load_guess.start()
    own_guess = pltpu.make_async_copy(g_ref.at[0], own, load_sem.at[1])
    own_start = pltpu.make_async_copy(q_ref, own, load_sem.at[1])
    first_start = pltpu.make_async_copy(q_ref, e2.at[:, mid, body, :], load_sem.at[2])
    pl.when(p < slabs - 1)(own_guess.start)
    pl.when(p == slabs - 1)(own_start.start)
    pl.when(p == 0)(first_start.start)

    barrier = pltpu.get_barrier_semaphore()

    def greet_space(d, carry):
        pl.semaphore_signal(barrier, inc=1, device_id={"space": lax.rem(s + d, n)}, device_id_type=MESH)
        return carry

    lax.fori_loop(1, n, greet_space, 0)
    for d in range(1, slabs):
        pl.semaphore_signal(barrier, inc=1, device_id={"tm": lax.rem(p + d, slabs)}, device_id_type=MESH)

    wide = rows + 2 * REACH
    border = jnp.zeros((TILE, nz), jnp.float32)

    def clear_pads(r, carry):
        for ref in (e1, e2, w1, w2):
            for c in range(comp):
                ref[c, r, pl.ds(0, TILE), :] = border
                ref[c, r, pl.ds(TILE + ny, TILE), :] = border
        return carry

    lax.fori_loop(0, wide, clear_pads, 0)

    def clear_rows(first):
        def one(t, carry):
            at = pl.ds(pl.multiple_of(TILE * t + TILE, TILE), TILE)
            for ref in (e1, e2):
                for c in range(comp):
                    for r in range(REACH):
                        ref[c, first + r, at, :] = border
            return carry

        lax.fori_loop(0, tiles, one, 0)

    pl.when(s == 0)(functools.partial(clear_rows, 0))
    pl.when(s == n - 1)(functools.partial(clear_rows, REACH + rows))

    left_inside = jnp.where(has_left, 1.0, 0.0).astype(jnp.float32)
    right_inside = jnp.where(has_right, 1.0, 0.0).astype(jnp.float32)

    def inside(r):
        if r < REACH:
            return left_inside
        if r >= REACH + rows:
            return right_inside
        return 1.0

    pl.semaphore_wait(barrier, n - 1 + slabs - 1)

    def halo(ref, send, recv, t):
        at = pl.ds(pl.multiple_of(TILE * t + TILE, TILE), TILE)
        source = ref.at[:, mid, at, :]
        to_left = pltpu.make_async_remote_copy(
            source, ref.at[:, pl.ds(REACH + rows, REACH), at, :], send.at[0, t], recv.at[0, t],
            device_id={"space": lax.rem(s + n - 1, n)}, device_id_type=MESH,
        )
        to_right = pltpu.make_async_remote_copy(
            source, ref.at[:, pl.ds(0, REACH), at, :], send.at[1, t], recv.at[1, t],
            device_id={"space": lax.rem(s + 1, n)}, device_id_type=MESH,
        )
        return to_left, to_right

    def halo_start(ref, send, recv, t):
        to_left, to_right = halo(ref, send, recv, t)
        pl.when(has_left)(to_left.start)
        pl.when(has_right)(to_right.start)

    def halo_arrived(ref, send, recv, t):
        to_left, to_right = halo(ref, send, recv, t)
        pl.when(has_right)(to_left.wait_recv)
        pl.when(has_left)(to_right.wait_recv)

    def halo_sent(ref, send, recv, t):
        to_left, to_right = halo(ref, send, recv, t)
        pl.when(has_left)(to_left.wait_send)
        pl.when(has_right)(to_right.wait_send)

    def over(lo, hi, act):
        def one(t, carry):
            act(t)
            return carry

        lax.fori_loop(lo, hi, one, 0)

    def to_second(t):
        at = pl.ds(pl.multiple_of(TILE * t, TILE), TILE)
        padded = pl.ds(pl.multiple_of(TILE * t + TILE, TILE), TILE)
        return pltpu.make_async_remote_copy(
            x.at[:, :, at, :], e2.at[:, mid, padded, :], x_send.at[t], s_recv.at[t],
            device_id={"tm": lax.rem(p + 2, slabs)}, device_id_type=MESH,
        )

    def to_relaxed(t):
        at = pl.ds(pl.multiple_of(TILE * t, TILE), TILE)
        return pltpu.make_async_remote_copy(
            x.at[:, :, at, :], relaxed.at[:, :, at, :], r_send.at[t], r_recv.at[t],
            device_id={"tm": lax.rem(p + 1, slabs)}, device_id_type=MESH,
        )

    def passed_on(t):
        at = pl.ds(pl.multiple_of(TILE * t, TILE), TILE)
        padded = pl.ds(pl.multiple_of(TILE * t + TILE, TILE), TILE)
        return pltpu.make_async_remote_copy(
            e2.at[:, mid, padded, :], relaxed.at[:, :, at, :], f_send.at[t], r_recv.at[t],
            device_id={"tm": lax.rem(p + slabs - 1, slabs)}, device_id_type=MESH,
        )

    sends_second = p != 2
    sends_relaxed = lax.rem(p, 2) == 0
    passes_on = p == slabs - 1

    pl.when(p < slabs - 1)(own_guess.wait)
    pl.when(p == slabs - 1)(own_start.wait)
    over(0, tiles, functools.partial(halo_start, e1, h1_send, h1_recv))

    def stage_one(k, carry):
        later = (k + CHUNKS - 1) // CHUNKS
        final = (k + 1) // CHUNKS
        ready = 2 * k + 4 - 2 * final
        over((2 * k + 2) * later, ready, functools.partial(halo_arrived, e1, h1_send, h1_recv))
        out_lo, out_hi = 2 * k + later, 2 * k + 3 - final
        phi(e1, x, w1, w2, src, inv, inside, rows, 2 * k, ready, out_lo, out_hi)

        def send(t):
            pl.when(sends_second)(lambda: to_second(t).start())
            pl.when(sends_relaxed)(lambda: to_relaxed(t).start())

        over(out_lo, out_hi, send)
        return carry

    lax.fori_loop(0, CHUNKS, stage_one, 0)

    pl.when(p == 0)(first_start.wait)

    def take(t):
        pl.when(p > 0)(lambda: to_second(t).wait_recv())
        halo_start(e2, h2_send, h2_recv, t)
        pl.when(passes_on)(lambda: passed_on(t).start())

    over(0, 3, take)

    def stage_two(k, carry):
        later = (k + CHUNKS - 1) // CHUNKS
        final = (k + 1) // CHUNKS
        next_final = (k + 2) // CHUNKS - final
        over(2 * k + 3 - final, 2 * k + 5 - next_final - 3 * final, take)
        ready = 2 * k + 3 - final
        over(2 * k + later, ready, functools.partial(halo_arrived, e2, h2_send, h2_recv))
        phi(e2, again, w1, w2, src, inv, inside, rows, 2 * k - later, ready, 2 * k, 2 * k + 2)
        return carry

    lax.fori_loop(0, CHUNKS, stage_two, 0)

    load_guess.wait()
    pl.when(p > 0)(lambda: over(0, tiles, lambda t: to_relaxed(t).wait_recv()))

    @pl.when(p == 0)
    def _():
        def one(t):
            at = pl.ds(pl.multiple_of(TILE * t, TILE), TILE)
            for c in range(comp):
                for r in range(rows):
                    relaxed[c, r, at, :] = again[c, r, at, :]

        over(0, tiles, one)

    def gather(t, totals):
        at = pl.ds(pl.multiple_of(TILE * t, TILE), TILE)
        totals = list(totals)
        for c in range(comp):
            for r in range(rows):
                value = again[c, r, at, :]
                totals[c] = totals[c] + (value - guess[c, r, at, :])
                rest[c, r, at, :] = value - relaxed[c, r, at, :]
        return tuple(totals)

    totals = lax.fori_loop(0, tiles, gather, tuple(border for _ in range(comp)))
    sums[s] = border
    for c in range(comp):
        sums[s, pl.ds(c, 1), :] = jnp.sum(totals[c], axis=0, keepdims=True)

    def share(d):
        return pltpu.make_async_remote_copy(
            sums.at[s], sums.at[s], sum_send.at[d], sum_recv.at[s],
            device_id={"space": lax.rem(s + d, n)}, device_id_type=MESH,
        )

    def shared_arrived(d):
        source = lax.rem(s + d, n)
        pltpu.make_async_remote_copy(
            sums.at[source], sums.at[source], sum_send.at[d], sum_recv.at[source],
            device_id={"space": source}, device_id_type=MESH,
        ).wait_recv()

    over(1, n, lambda d: share(d).start())
    out_rest = pltpu.make_async_copy(rest, residual_ref.at[0], out_sem.at[0])
    out_rest.start()
    over(1, n, shared_arrived)
    total = lax.fori_loop(0, n, lambda i, held: held + sums[i], border)

    lane = lax.broadcasted_iota(jnp.int32, (TILE, nz), 1)
    width = 1
    while width < BLK:
        upper = pltpu.roll(total, nz - width, 1)
        lower = pltpu.roll(total, width, 1)
        total = total + jnp.where((lane // width) % 2 == 0, upper, lower)
        width *= 2
    terms[p] = total * (1.0 / (rows * n * ny * BLK))

    def tell(d):
        return pltpu.make_async_remote_copy(
            terms.at[p], terms.at[p], term_send.at[d], term_recv.at[p],
            device_id={"tm": lax.rem(p + d, slabs)}, device_id_type=MESH,
        )

    for d in range(1, slabs):
        tell(d).start()
    for d in range(1, slabs):
        source = lax.rem(p + d, slabs)
        pltpu.make_async_remote_copy(
            terms.at[source], terms.at[source], term_send.at[d], term_recv.at[source],
            device_id={"tm": source}, device_id_type=MESH,
        ).wait_recv()

    decay = 1.0 / (1.0 + STEPS_SLAB * time_step * linear_rate)
    error = terms[0]
    for j in range(1, slabs):
        error = jnp.where(p >= j, decay * error + terms[j], error)
    spread = [jnp.broadcast_to(error[c : c + 1], (TILE, nz)) for c in range(comp)]

    def correct(t):
        at = pl.ds(pl.multiple_of(TILE * t, TILE), TILE)
        for c in range(comp):
            for r in range(rows):
                result[c, r, at, :] = relaxed[c, r, at, :] + spread[c]

    over(0, tiles, correct)
    out_result = pltpu.make_async_copy(result, corrected_ref.at[0], out_sem.at[1])
    out_result.start()

    def sent(t):
        halo_sent(e1, h1_send, h1_recv, t)
        halo_sent(e2, h2_send, h2_recv, t)
        pl.when(sends_second)(lambda: to_second(t).wait_send())
        pl.when(sends_relaxed)(lambda: to_relaxed(t).wait_send())
        pl.when(passes_on)(lambda: passed_on(t).wait_send())

    over(0, tiles, sent)
    over(1, n, lambda d: share(d).wait_send())
    for d in range(1, slabs):
        tell(d).wait_send()
    out_rest.wait()
    out_result.wait()


def per_device(n, slabs, q_start, guess):
    comp, rows, ny, nz = q_start.shape
    tiles = ny // TILE
    wide = rows + 2 * REACH
    vmem = lambda *shape: pltpu.VMEM(shape, jnp.float32)
    sems = lambda *shape: pltpu.SemaphoreType.DMA(shape)
    padded = (wide, ny + 2 * TILE, nz)
    block = (comp, rows, ny, nz)
    return pl.pallas_call(
        functools.partial(kernel, n, slabs),
        out_shape=(jax.ShapeDtypeStruct(guess.shape, jnp.float32),) * 2,
        in_specs=[pl.BlockSpec(memory_space=pl.ANY)] * 2,
        out_specs=(pl.BlockSpec(memory_space=pl.ANY),) * 2,
        scratch_shapes=[
            vmem(comp, *padded), vmem(comp, *padded), vmem(comp, *padded), vmem(comp, *padded),
            vmem(comp, *padded), vmem(*padded),
            vmem(*block), vmem(*block), vmem(*block), vmem(*block), vmem(*block), vmem(*block),
            vmem(n, TILE, nz), vmem(slabs, TILE, nz),
            sems(3), sems(2, tiles), sems(2, tiles), sems(2, tiles), sems(2, tiles),
            sems(tiles), sems(tiles), sems(tiles), sems(tiles), sems(tiles),
            sems(n), sems(n), sems(slabs), sems(slabs), sems(2),
        ],
        compiler_params=pltpu.CompilerParams(
            collective_id=0, has_side_effects=True, vmem_limit_bytes=32 * 1024 * 1024
        ),
    )(q_start, guess)


def solution(mesh):
    return jax.shard_map(
        functools.partial(per_device, mesh.shape["space"], mesh.shape["tm"]),
        mesh=mesh,
        in_specs=(P(None, "space", None, None), P("tm", None, "space", None, None)),
        out_specs=(P("tm", None, "space", None, None), P("tm", None, "space", None, None)),
        check_vma=False,
    )
```

```python
import functools

import jax
import jax.numpy as jnp
from jax import lax
from jax.experimental import pallas as pl
from jax.experimental.pallas import tpu as pltpu
from jax.sharding import PartitionSpec as P

STEPS_SLAB = 2
SWEEPS = 2
BLK = 4

time_step = 0.1
cross = 8.0
axial = 2.0
linear_rate = 0.1
quadratic_rate = 0.5
cubic_rate = 1.0

REACH = STEPS_SLAB * SWEEPS
TILE = 8
CHUNKS = 4
MESH = pl.DeviceIdType.MESH


def bulk(field):
    a, b, c, d, e = field
    f = -a - d
    aa, bb, cc, dd, ee, ff = a * a, b * b, c * c, d * d, e * e, f * f
    trace = aa + dd + ff + 2.0 * (bb + cc + ee)
    third = trace * (1.0 / 3.0)
    quad = (
        aa + bb + cc - third,
        a * b + b * d + c * e,
        a * c + b * e + c * f,
        bb + dd + ee - third,
        b * c + d * e + e * f,
    )
    source = [q + (time_step * quadratic_rate) * s for q, s in zip(field, quad)]
    constant = 1.0 + time_step * linear_rate + 2.0 * (2.0 * cross + axial)
    diagonal = constant + (time_step * cubic_rate) * trace
    return source, diagonal


def neighbours(ref, c, r, t, before, now, after, edge=False):
    along_x = before + after
    if edge:
        higher = pltpu.roll(now, TILE - 1, 0)
    else:
        higher = ref[c, r, pl.ds(TILE * t + TILE + 1, TILE), :]
    along_y = ref[c, r, pl.ds(TILE * t + TILE - 1, TILE), :] + higher
    lanes = now.shape[1]
    along_z = pltpu.roll(now, 1, 1) + pltpu.roll(now, lanes - 1, 1)
    return (cross / axial) * (along_x + along_y) + along_z


def tile_rows(ref, r, t):
    at = pl.ds(pl.multiple_of(TILE * t + TILE, TILE), TILE)
    return [ref[c, r, at, :] for c in range(ref.shape[0])]


def first_sweep(ref, out, src, inv, rows, inside, lo, hi, partial):
    comp = ref.shape[0]
    tiles = ref.shape[2] // TILE - 2

    def one(edge, t, carry):
        at = pl.ds(pl.multiple_of(TILE * t + TILE, TILE), TILE)
        before, now = tile_rows(ref, rows[0] - 1, t), tile_rows(ref, rows[0], t)
        for r in rows:
            after = tile_rows(ref, r + 1, t)
            source, diagonal = bulk(now)
            inverse = inside(r) / diagonal
            scaled = axial * inverse
            inv[r, at, :] = scaled
            for c in range(comp):
                part = source[c] * inverse
                src[c, r, at, :] = part
                out[c, r, at, :] = part + scaled * neighbours(
                    ref, c, r, t, before[c], now[c], after[c], edge
                )
            before, now = now, after
        return carry

    if not partial:
        lax.fori_loop(lo, hi, functools.partial(one, False), 0)
        return
    last = hi - 1 + lax.div(hi, tiles)
    lax.fori_loop(lo, last, functools.partial(one, False), 0)
    lax.fori_loop(last, hi, functools.partial(one, True), 0)


def next_sweep(ref, store, src, inv, rows, lo, hi):
    comp = ref.shape[0]

    def one(t, carry):
        at = pl.ds(pl.multiple_of(TILE * t + TILE, TILE), TILE)
        before, now = tile_rows(ref, rows[0] - 1, t), tile_rows(ref, rows[0], t)
        for r in rows:
            after = tile_rows(ref, r + 1, t)
            scaled = inv[r, at, :]
            for c in range(comp):
                store(c, r, t, src[c, r, at, :] + scaled * neighbours(ref, c, r, t, before[c], now[c], after[c]))
            before, now = now, after
        return carry

    lax.fori_loop(lo, hi, one, 0)


def phi(ref, out, w1, w2, src, inv, inside, rows, lo, hi, out_lo, out_hi):
    wide = rows + 2 * REACH

    def keep(c, r, t, value):
        w2[c, r, pl.ds(pl.multiple_of(TILE * t + TILE, TILE), TILE), :] = value

    def last(c, r, t, value):
        out[c, r - REACH, pl.ds(pl.multiple_of(TILE * t, TILE), TILE), :] = value

    first_sweep(ref, w1, src, inv, range(1, wide - 1), inside, lo, hi, True)
    next_sweep(w1, keep, src, inv, range(2, wide - 2), lo, hi)
    first_sweep(w2, w1, src, inv, range(3, wide - 3), inside, lo, hi, False)
    next_sweep(w1, last, src, inv, range(4, wide - 4), out_lo, out_hi)


def kernel(
    n, slabs, q_ref, g_ref, relaxed_ref, again_ref, error_ref,
    e1, e2, w1, w2, src, inv, x, again, relaxed, guess, sums, terms,
    load_sem, h1_send, h1_recv, h2_send, h2_recv, x_send, r_send, f_send, s_recv, r_recv,
    sum_send, sum_recv, term_send, term_recv, out_sem,
):
    p = lax.axis_index("tm")
    s = lax.axis_index("space")
    comp, rows, ny, nz = x.shape
    tiles = ny // TILE
    mid = pl.ds(REACH, rows)
    body = pl.ds(TILE, ny)
    has_left, has_right = s > 0, s < n - 1

    barrier = pltpu.get_barrier_semaphore()

    def greet_space(d, carry):
        pl.semaphore_signal(barrier, inc=1, device_id={"space": lax.rem(s + d, n)}, device_id_type=MESH)
        return carry

    lax.fori_loop(1, n, greet_space, 0)
    for d in range(1, slabs):
        pl.semaphore_signal(barrier, inc=1, device_id={"tm": lax.rem(p + d, slabs)}, device_id_type=MESH)

    own = e1.at[:, mid, body, :]
    load_guess = pltpu.make_async_copy(g_ref.at[0], guess, load_sem.at[0])
    load_guess.start()
    own_guess = pltpu.make_async_copy(g_ref.at[0], own, load_sem.at[1])
    own_start = pltpu.make_async_copy(q_ref, own, load_sem.at[1])
    first_start = pltpu.make_async_copy(q_ref, e2.at[:, mid, body, :], load_sem.at[2])
    pl.when(p < slabs - 1)(own_guess.start)
    pl.when(p == slabs - 1)(own_start.start)
    pl.when(p == 0)(first_start.start)

    wide = rows + 2 * REACH
    border = jnp.zeros((TILE, nz), jnp.float32)

    def clear_pads(r, carry):
        for ref in (e1, e2, w1, w2):
            for c in range(comp):
                ref[c, r, pl.ds(0, TILE), :] = border
                ref[c, r, pl.ds(TILE + ny, TILE), :] = border
        return carry

    lax.fori_loop(0, wide, clear_pads, 0)

    def clear_rows(first):
        def one(t, carry):
            at = pl.ds(pl.multiple_of(TILE * t + TILE, TILE), TILE)
            for ref in (e1, e2):
                for c in range(comp):
                    for r in range(REACH):
                        ref[c, first + r, at, :] = border
            return carry

        lax.fori_loop(0, tiles, one, 0)

    pl.when(s == 0)(functools.partial(clear_rows, 0))
    pl.when(s == n - 1)(functools.partial(clear_rows, REACH + rows))

    left_inside = jnp.where(has_left, 1.0, 0.0).astype(jnp.float32)
    right_inside = jnp.where(has_right, 1.0, 0.0).astype(jnp.float32)

    def inside(r):
        if r < REACH:
            return left_inside
        if r >= REACH + rows:
            return right_inside
        return 1.0

    pl.semaphore_wait(barrier, n - 1 + slabs - 1)

    def halo(ref, send, recv, t):
        at = pl.ds(pl.multiple_of(TILE * t + TILE, TILE), TILE)
        source = ref.at[:, mid, at, :]
        to_left = pltpu.make_async_remote_copy(
            source, ref.at[:, pl.ds(REACH + rows, REACH), at, :], send.at[0, t], recv.at[0, t],
            device_id={"space": lax.rem(s + n - 1, n)}, device_id_type=MESH,
        )
        to_right = pltpu.make_async_remote_copy(
            source, ref.at[:, pl.ds(0, REACH), at, :], send.at[1, t], recv.at[1, t],
            device_id={"space": lax.rem(s + 1, n)}, device_id_type=MESH,
        )
        return to_left, to_right

    def halo_start(ref, send, recv, t):
        to_left, to_right = halo(ref, send, recv, t)
        pl.when(has_left)(to_left.start)
        pl.when(has_right)(to_right.start)

    def halo_arrived(ref, send, recv, t):
        to_left, to_right = halo(ref, send, recv, t)
        pl.when(has_right)(to_left.wait_recv)
        pl.when(has_left)(to_right.wait_recv)

    def halo_sent(ref, send, recv, t):
        to_left, to_right = halo(ref, send, recv, t)
        pl.when(has_left)(to_left.wait_send)
        pl.when(has_right)(to_right.wait_send)

    def over(lo, hi, act):
        def one(t, carry):
            act(t)
            return carry

        lax.fori_loop(lo, hi, one, 0)

    def to_second(t):
        at = pl.ds(pl.multiple_of(TILE * t, TILE), TILE)
        padded = pl.ds(pl.multiple_of(TILE * t + TILE, TILE), TILE)
        return pltpu.make_async_remote_copy(
            x.at[:, :, at, :], e2.at[:, mid, padded, :], x_send.at[t], s_recv.at[t],
            device_id={"tm": lax.rem(p + 2, slabs)}, device_id_type=MESH,
        )

    def to_relaxed(t):
        at = pl.ds(pl.multiple_of(TILE * t, TILE), TILE)
        return pltpu.make_async_remote_copy(
            x.at[:, :, at, :], relaxed.at[:, :, at, :], r_send.at[t], r_recv.at[t],
            device_id={"tm": lax.rem(p + 1, slabs)}, device_id_type=MESH,
        )

    def passed_on(t):
        at = pl.ds(pl.multiple_of(TILE * t, TILE), TILE)
        padded = pl.ds(pl.multiple_of(TILE * t + TILE, TILE), TILE)
        return pltpu.make_async_remote_copy(
            e2.at[:, mid, padded, :], relaxed.at[:, :, at, :], f_send.at[t], r_recv.at[t],
            device_id={"tm": lax.rem(p + slabs - 1, slabs)}, device_id_type=MESH,
        )

    sends_second = p != 2
    sends_relaxed = lax.rem(p, 2) == 0
    passes_on = p == slabs - 1

    pl.when(p < slabs - 1)(own_guess.wait)
    pl.when(p == slabs - 1)(own_start.wait)
    over(0, tiles, functools.partial(halo_start, e1, h1_send, h1_recv))

    def stage_one(k, carry):
        later = (k + CHUNKS) // (CHUNKS + 1)
        final = k // CHUNKS
        ready = 2 * k + 2 - 2 * final
        over(2 * k * later, ready, functools.partial(halo_arrived, e1, h1_send, h1_recv))
        out_lo, out_hi = 2 * k - later, 2 * k + 1 - final
        phi(e1, x, w1, w2, src, inv, inside, rows, 2 * k - 2 * later, ready, out_lo, out_hi)

        def send(t):
            pl.when(sends_second)(lambda: to_second(t).start())
            pl.when(sends_relaxed)(lambda: to_relaxed(t).start())

        over(out_lo, out_hi, send)
        return carry

    lax.fori_loop(0, CHUNKS + 1, stage_one, 0)

    pl.when(p == 0)(first_start.wait)

    def take(t):
        pl.when(p > 0)(lambda: to_second(t).wait_recv())
        halo_start(e2, h2_send, h2_recv, t)
        pl.when(passes_on)(lambda: passed_on(t).start())

    over(0, 3, take)

    def stage_two(k, totals):
        later = (k + CHUNKS - 1) // CHUNKS
        final = (k + 1) // CHUNKS
        next_final = (k + 2) // CHUNKS - final
        over(2 * k + 3 - final, 2 * k + 5 - next_final - 3 * final, take)
        ready = 2 * k + 3 - final
        over(2 * k + later, ready, functools.partial(halo_arrived, e2, h2_send, h2_recv))
        phi(e2, again, w1, w2, src, inv, inside, rows, 2 * k - later, ready, 2 * k, 2 * k + 2)
        return lax.fori_loop(2 * k, 2 * k + 2, gather, totals)

    def gather(t, totals):
        at = pl.ds(pl.multiple_of(TILE * t, TILE), TILE)
        return tuple(
            total + sum(again[c, r, at, :] - guess[c, r, at, :] for r in range(rows))
            for c, total in enumerate(totals)
        )

    load_guess.wait()
    totals = lax.fori_loop(0, CHUNKS, stage_two, tuple(border for _ in range(comp)))
    sums[s] = border
    for c in range(comp):
        sums[s, pl.ds(c, 1), :] = jnp.sum(totals[c], axis=0, keepdims=True)

    def share(d):
        return pltpu.make_async_remote_copy(
            sums.at[s], sums.at[s], sum_send.at[d], sum_recv.at[s],
            device_id={"space": lax.rem(s + d, n)}, device_id_type=MESH,
        )

    def shared_arrived(d):
        source = lax.rem(s + d, n)
        pltpu.make_async_remote_copy(
            sums.at[source], sums.at[source], sum_send.at[d], sum_recv.at[source],
            device_id={"space": source}, device_id_type=MESH,
        ).wait_recv()

    over(1, n, lambda d: share(d).start())
    out_again = pltpu.make_async_copy(again, again_ref, out_sem.at[0])
    out_again.start()
    pl.when(p > 0)(lambda: over(0, tiles, lambda t: to_relaxed(t).wait_recv()))
    out_first = pltpu.make_async_copy(again, relaxed_ref, out_sem.at[1])
    out_relaxed = pltpu.make_async_copy(relaxed, relaxed_ref, out_sem.at[1])
    pl.when(p == 0)(out_first.start)
    pl.when(p > 0)(out_relaxed.start)
    over(1, n, shared_arrived)
    total = lax.fori_loop(0, n, lambda i, held: held + sums[i], border)

    lane = lax.broadcasted_iota(jnp.int32, (TILE, nz), 1)
    width = 1
    while width < BLK:
        upper = pltpu.roll(total, nz - width, 1)
        lower = pltpu.roll(total, width, 1)
        total = total + jnp.where((lane // width) % 2 == 0, upper, lower)
        width *= 2
    terms[p] = total * (1.0 / (rows * n * ny * BLK))

    def tell(d):
        return pltpu.make_async_remote_copy(
            terms.at[p], terms.at[p], term_send.at[d], term_recv.at[p],
            device_id={"tm": lax.rem(p + d, slabs)}, device_id_type=MESH,
        )

    for d in range(1, slabs):
        tell(d).start()
    for d in range(1, slabs):
        source = lax.rem(p + d, slabs)
        pltpu.make_async_remote_copy(
            terms.at[source], terms.at[source], term_send.at[d], term_recv.at[source],
            device_id={"tm": source}, device_id_type=MESH,
        ).wait_recv()

    decay = 1.0 / (1.0 + STEPS_SLAB * time_step * linear_rate)
    error = terms[0]
    for j in range(1, slabs):
        error = jnp.where(p >= j, decay * error + terms[j], error)
    error_ref[...] = error

    def sent(t):
        halo_sent(e1, h1_send, h1_recv, t)
        halo_sent(e2, h2_send, h2_recv, t)
        pl.when(sends_second)(lambda: to_second(t).wait_send())
        pl.when(sends_relaxed)(lambda: to_relaxed(t).wait_send())
        pl.when(passes_on)(lambda: passed_on(t).wait_send())

    over(0, tiles, sent)
    over(1, n, lambda d: share(d).wait_send())
    for d in range(1, slabs):
        tell(d).wait_send()
    out_again.wait()
    pl.when(p == 0)(out_first.wait)
    pl.when(p > 0)(out_relaxed.wait)


def per_device(n, slabs, q_start, guess):
    comp, rows, ny, nz = q_start.shape
    tiles = ny // TILE
    wide = rows + 2 * REACH
    vmem = lambda *shape: pltpu.VMEM(shape, jnp.float32)
    sems = lambda *shape: pltpu.SemaphoreType.DMA(shape)
    padded = (wide, ny + 2 * TILE, nz)
    block = (comp, rows, ny, nz)
    relaxed, again, error = pl.pallas_call(
        functools.partial(kernel, n, slabs),
        out_shape=(jax.ShapeDtypeStruct(block, jnp.float32),) * 2
        + (jax.ShapeDtypeStruct((TILE, nz), jnp.float32),),
        in_specs=[pl.BlockSpec(memory_space=pl.ANY)] * 2,
        out_specs=(pl.BlockSpec(memory_space=pl.ANY),) * 2 + (pl.BlockSpec(memory_space=pltpu.VMEM),),
        scratch_shapes=[
            vmem(comp, *padded), vmem(comp, *padded), vmem(comp, *padded), vmem(comp, *padded),
            vmem(comp, *padded), vmem(*padded),
            vmem(*block), vmem(*block), vmem(*block), vmem(*block),
            vmem(n, TILE, nz), vmem(slabs, TILE, nz),
            sems(3), sems(2, tiles), sems(2, tiles), sems(2, tiles), sems(2, tiles),
            sems(tiles), sems(tiles), sems(tiles), sems(tiles), sems(tiles),
            sems(n), sems(n), sems(slabs), sems(slabs), sems(2),
        ],
        compiler_params=pltpu.CompilerParams(
            collective_id=0, has_side_effects=True, vmem_limit_bytes=60 * 1024 * 1024
        ),
    )(q_start, guess)
    corrected = relaxed + error[:comp, None, None, :]
    residual = again - relaxed
    return corrected[None], residual[None]


def solution(mesh):
    return jax.shard_map(
        functools.partial(per_device, mesh.shape["space"], mesh.shape["tm"]),
        mesh=mesh,
        in_specs=(P(None, "space", None, None), P("tm", None, "space", None, None)),
        out_specs=(P("tm", None, "space", None, None), P("tm", None, "space", None, None)),
        check_vma=False,
    )
```

```python
import functools

import jax
import jax.numpy as jnp
from jax import lax
from jax.experimental import pallas as pl
from jax.experimental.pallas import tpu as pltpu
from jax.sharding import PartitionSpec as P

STEPS_SLAB = 2
SWEEPS = 2
BLK = 4

time_step = 0.1
cross = 8.0
axial = 2.0
linear_rate = 0.1
quadratic_rate = 0.5
cubic_rate = 1.0

REACH = STEPS_SLAB * SWEEPS
TILE = 8
MESH = pl.DeviceIdType.MESH


def bulk(field):
    a, b, c, d, e = field
    f = -a - d
    aa, bb, cc, dd, ee, ff = a * a, b * b, c * c, d * d, e * e, f * f
    trace = aa + dd + ff + 2.0 * (bb + cc + ee)
    third = trace * (1.0 / 3.0)
    quad = (
        aa + bb + cc - third,
        a * b + b * d + c * e,
        a * c + b * e + c * f,
        bb + dd + ee - third,
        b * c + d * e + e * f,
    )
    source = [q + (time_step * quadratic_rate) * s for q, s in zip(field, quad)]
    constant = 1.0 + time_step * linear_rate + 2.0 * (2.0 * cross + axial)
    diagonal = constant + (time_step * cubic_rate) * trace
    return source, diagonal


def neighbours(ref, c, r, t, before, now, after):
    along_x = before + after
    along_y = ref[c, r, pl.ds(TILE * t + TILE - 1, TILE), :] + ref[c, r, pl.ds(TILE * t + TILE + 1, TILE), :]
    lanes = now.shape[1]
    along_z = pltpu.roll(now, 1, 1) + pltpu.roll(now, lanes - 1, 1)
    return (cross / axial) * (along_x + along_y) + along_z


def padded_at(t):
    return pl.ds(pl.multiple_of(TILE * t + TILE, TILE), TILE)


def tile_rows(ref, r, t):
    return [ref[c, r, padded_at(t), :] for c in range(ref.shape[0])]


def first_sweep(ref, out, src, inv, rows, inside, t):
    at = padded_at(t)
    before, now = tile_rows(ref, rows[0] - 1, t), tile_rows(ref, rows[0], t)
    for r in rows:
        after = tile_rows(ref, r + 1, t)
        source, diagonal = bulk(now)
        inverse = inside(r) / diagonal
        scaled = axial * inverse
        inv[r, at, :] = scaled
        for c in range(ref.shape[0]):
            part = source[c] * inverse
            src[c, r, at, :] = part
            out[c, r, at, :] = part + scaled * neighbours(ref, c, r, t, before[c], now[c], after[c])
        before, now = now, after


def next_sweep(ref, store, src, inv, rows, t):
    at = padded_at(t)
    before, now = tile_rows(ref, rows[0] - 1, t), tile_rows(ref, rows[0], t)
    for r in rows:
        after = tile_rows(ref, r + 1, t)
        scaled = inv[r, at, :]
        for c in range(ref.shape[0]):
            store(c, r, t, src[c, r, at, :] + scaled * neighbours(ref, c, r, t, before[c], now[c], after[c]))
        before, now = now, after


def phi(ref, out, w1, w2, w3, src, inv, inside, rows, tiles, arrive, finish, carry):
    wide = rows + 2 * REACH

    def keep(c, r, t, value):
        w2[c, r, padded_at(t), :] = value

    def last(c, r, t, value):
        out[c, r - REACH, pl.ds(pl.multiple_of(TILE * t, TILE), TILE), :] = value

    sweeps = (
        lambda t: first_sweep(ref, w1, src, inv, range(1, wide - 1), inside, t),
        lambda t: next_sweep(w1, keep, src, inv, range(2, wide - 2), t),
        lambda t: first_sweep(w2, w3, src, inv, range(3, wide - 3), inside, t),
        lambda t: next_sweep(w3, last, src, inv, range(4, wide - 4), t),
    )

    def turn(i, carry):
        pl.when(i < tiles)(lambda: arrive(i))
        for lag, sweep in enumerate(sweeps):
            here = jnp.logical_and(i >= lag + 1, i < tiles + lag + 1)
            pl.when(here)(functools.partial(sweep, i - lag - 1))
        low = jnp.where(i < REACH, 0, i - REACH)
        high = jnp.where(i < REACH, 0, i - REACH + 1)
        return lax.fori_loop(low, high, finish, carry)

    return lax.fori_loop(0, tiles + REACH, turn, carry)


def kernel(
    n, slabs, q_ref, g_ref, corrected_ref, residual_ref,
    e1, e2, w1, w2, w3, src, inv, x, again, relaxed, guess, result, rest, sums, terms,
    load_sem, h1_send, h1_recv, h2_send, h2_recv, x_send, r_send, f_send, s_recv, r_recv,
    sum_send, sum_recv, term_send, term_recv, rest_sem, out_sem,
):
    p = lax.axis_index("tm")
    s = lax.axis_index("space")
    comp, rows, ny, nz = x.shape
    tiles = ny // TILE
    mid = pl.ds(REACH, rows)
    body = pl.ds(TILE, ny)
    has_left, has_right = s > 0, s < n - 1

    barrier = pltpu.get_barrier_semaphore()

    def greet_space(d, carry):
        pl.semaphore_signal(barrier, inc=1, device_id={"space": lax.rem(s + d, n)}, device_id_type=MESH)
        return carry

    lax.fori_loop(1, n, greet_space, 0)
    for d in range(1, slabs):
        pl.semaphore_signal(barrier, inc=1, device_id={"tm": lax.rem(p + d, slabs)}, device_id_type=MESH)

    own = e1.at[:, mid, body, :]
    load_guess = pltpu.make_async_copy(g_ref.at[0], guess, load_sem.at[0])
    load_guess.start()
    own_guess = pltpu.make_async_copy(g_ref.at[0], own, load_sem.at[1])
    own_start = pltpu.make_async_copy(q_ref, own, load_sem.at[1])
    first_start = pltpu.make_async_copy(q_ref, e2.at[:, mid, body, :], load_sem.at[2])
    pl.when(p < slabs - 1)(own_guess.start)
    pl.when(p == slabs - 1)(own_start.start)
    pl.when(p == 0)(first_start.start)

    wide = rows + 2 * REACH
    border = jnp.zeros((TILE, nz), jnp.float32)

    def clear_pads(r, carry):
        for ref in (e1, e2, w1, w2, w3):
            for c in range(comp):
                ref[c, r, pl.ds(0, TILE), :] = border
                ref[c, r, pl.ds(TILE + ny, TILE), :] = border
        return carry

    lax.fori_loop(0, wide, clear_pads, 0)

    def clear_rows(first):
        def one(t, carry):
            at = pl.ds(pl.multiple_of(TILE * t + TILE, TILE), TILE)
            for ref in (e1, e2):
                for c in range(comp):
                    for r in range(REACH):
                        ref[c, first + r, at, :] = border
            return carry

        lax.fori_loop(0, tiles, one, 0)

    pl.when(s == 0)(functools.partial(clear_rows, 0))
    pl.when(s == n - 1)(functools.partial(clear_rows, REACH + rows))

    left_inside = jnp.where(has_left, 1.0, 0.0).astype(jnp.float32)
    right_inside = jnp.where(has_right, 1.0, 0.0).astype(jnp.float32)

    def inside(r):
        if r < REACH:
            return left_inside
        if r >= REACH + rows:
            return right_inside
        return 1.0

    pl.semaphore_wait(barrier, n - 1 + slabs - 1)

    def halo(ref, send, recv, t):
        at = pl.ds(pl.multiple_of(TILE * t + TILE, TILE), TILE)
        source = ref.at[:, mid, at, :]
        to_left = pltpu.make_async_remote_copy(
            source, ref.at[:, pl.ds(REACH + rows, REACH), at, :], send.at[0, t], recv.at[0, t],
            device_id={"space": lax.rem(s + n - 1, n)}, device_id_type=MESH,
        )
        to_right = pltpu.make_async_remote_copy(
            source, ref.at[:, pl.ds(0, REACH), at, :], send.at[1, t], recv.at[1, t],
            device_id={"space": lax.rem(s + 1, n)}, device_id_type=MESH,
        )
        return to_left, to_right

    def halo_start(ref, send, recv, t):
        to_left, to_right = halo(ref, send, recv, t)
        pl.when(has_left)(to_left.start)
        pl.when(has_right)(to_right.start)

    def halo_arrived(ref, send, recv, t):
        to_left, to_right = halo(ref, send, recv, t)
        pl.when(has_right)(to_left.wait_recv)
        pl.when(has_left)(to_right.wait_recv)

    def halo_sent(ref, send, recv, t):
        to_left, to_right = halo(ref, send, recv, t)
        pl.when(has_left)(to_left.wait_send)
        pl.when(has_right)(to_right.wait_send)

    def over(lo, hi, act):
        def one(t, carry):
            act(t)
            return carry

        lax.fori_loop(lo, hi, one, 0)

    def to_second(t):
        at = pl.ds(pl.multiple_of(TILE * t, TILE), TILE)
        padded = pl.ds(pl.multiple_of(TILE * t + TILE, TILE), TILE)
        return pltpu.make_async_remote_copy(
            x.at[:, :, at, :], e2.at[:, mid, padded, :], x_send.at[t], s_recv.at[t],
            device_id={"tm": lax.rem(p + 2, slabs)}, device_id_type=MESH,
        )

    def to_relaxed(t):
        at = pl.ds(pl.multiple_of(TILE * t, TILE), TILE)
        return pltpu.make_async_remote_copy(
            x.at[:, :, at, :], relaxed.at[:, :, at, :], r_send.at[t], r_recv.at[t],
            device_id={"tm": lax.rem(p + 1, slabs)}, device_id_type=MESH,
        )

    def passed_on(t):
        at = pl.ds(pl.multiple_of(TILE * t, TILE), TILE)
        padded = pl.ds(pl.multiple_of(TILE * t + TILE, TILE), TILE)
        return pltpu.make_async_remote_copy(
            e2.at[:, mid, padded, :], relaxed.at[:, :, at, :], f_send.at[t], r_recv.at[t],
            device_id={"tm": lax.rem(p + slabs - 1, slabs)}, device_id_type=MESH,
        )

    sends_second = p != 2
    sends_relaxed = lax.rem(p, 2) == 0
    passes_on = p == slabs - 1

    pl.when(p < slabs - 1)(own_guess.wait)
    pl.when(p == slabs - 1)(own_start.wait)
    over(0, tiles, functools.partial(halo_start, e1, h1_send, h1_recv))

    def send(t, carry):
        pl.when(sends_second)(lambda: to_second(t).start())
        pl.when(sends_relaxed)(lambda: to_relaxed(t).start())
        return carry

    phi(
        e1, x, w1, w2, w3, src, inv, inside, rows, tiles,
        functools.partial(halo_arrived, e1, h1_send, h1_recv), send, 0,
    )

    pl.when(p == 0)(first_start.wait)

    def take(t):
        pl.when(p > 0)(lambda: to_second(t).wait_recv())
        halo_start(e2, h2_send, h2_recv, t)
        pl.when(passes_on)(lambda: passed_on(t).start())

    def arrive(t):
        pl.when(t < tiles - 1)(lambda: take(t + 1))
        halo_arrived(e2, h2_send, h2_recv, t)

    def gather(t, totals):
        at = pl.ds(pl.multiple_of(TILE * t, TILE), TILE)
        return tuple(
            total + sum(again[c, r, at, :] - guess[c, r, at, :] for r in range(rows))
            for c, total in enumerate(totals)
        )

    load_guess.wait()
    take(0)
    totals = phi(
        e2, again, w1, w2, w3, src, inv, inside, rows, tiles,
        arrive, gather, tuple(border for _ in range(comp)),
    )
    sums[s] = border
    for c in range(comp):
        sums[s, pl.ds(c, 1), :] = jnp.sum(totals[c], axis=0, keepdims=True)

    def share(d):
        return pltpu.make_async_remote_copy(
            sums.at[s], sums.at[s], sum_send.at[d], sum_recv.at[s],
            device_id={"space": lax.rem(s + d, n)}, device_id_type=MESH,
        )

    def shared_arrived(d):
        source = lax.rem(s + d, n)
        pltpu.make_async_remote_copy(
            sums.at[source], sums.at[source], sum_send.at[d], sum_recv.at[source],
            device_id={"space": source}, device_id_type=MESH,
        ).wait_recv()

    over(1, n, lambda d: share(d).start())
    pl.when(p > 0)(lambda: over(0, tiles, lambda t: to_relaxed(t).wait_recv()))

    @pl.when(p == 0)
    def _():
        def same(t):
            at = pl.ds(pl.multiple_of(TILE * t, TILE), TILE)
            relaxed[:, :, at, :] = again[:, :, at, :]

        over(0, tiles, same)

    def subtract(t):
        at = pl.ds(pl.multiple_of(TILE * t, TILE), TILE)
        rest[:, :, at, :] = again[:, :, at, :] - relaxed[:, :, at, :]

    over(0, tiles, subtract)
    out_rest = pltpu.make_async_copy(rest, residual_ref.at[0], rest_sem.at[0])
    out_rest.start()
    over(1, n, shared_arrived)
    total = lax.fori_loop(0, n, lambda i, held: held + sums[i], border)

    lane = lax.broadcasted_iota(jnp.int32, (TILE, nz), 1)
    width = 1
    while width < BLK:
        upper = pltpu.roll(total, nz - width, 1)
        lower = pltpu.roll(total, width, 1)
        total = total + jnp.where((lane // width) % 2 == 0, upper, lower)
        width *= 2
    terms[p] = total * (1.0 / (rows * n * ny * BLK))

    def tell(d):
        return pltpu.make_async_remote_copy(
            terms.at[p], terms.at[p], term_send.at[d], term_recv.at[p],
            device_id={"tm": lax.rem(p + d, slabs)}, device_id_type=MESH,
        )

    for d in range(1, slabs):
        tell(d).start()
    for d in range(1, slabs):
        source = lax.rem(p + d, slabs)
        pltpu.make_async_remote_copy(
            terms.at[source], terms.at[source], term_send.at[d], term_recv.at[source],
            device_id={"tm": source}, device_id_type=MESH,
        ).wait_recv()

    decay = 1.0 / (1.0 + STEPS_SLAB * time_step * linear_rate)
    error = terms[0]
    for j in range(1, slabs):
        error = jnp.where(p >= j, decay * error + terms[j], error)
    spread = [jnp.broadcast_to(error[c : c + 1], (TILE, nz)) for c in range(comp)]

    def out_result(t):
        at = pl.ds(pl.multiple_of(TILE * t, TILE), TILE)
        return pltpu.make_async_copy(result.at[:, :, at, :], corrected_ref.at[0, :, :, at, :], out_sem.at[t])

    def correct(t):
        at = pl.ds(pl.multiple_of(TILE * t, TILE), TILE)
        for c in range(comp):
            for r in range(rows):
                result[c, r, at, :] = relaxed[c, r, at, :] + spread[c]
        out_result(t).start()

    over(0, tiles, correct)

    def sent(t):
        halo_sent(e1, h1_send, h1_recv, t)
        halo_sent(e2, h2_send, h2_recv, t)
        pl.when(sends_second)(lambda: to_second(t).wait_send())
        pl.when(sends_relaxed)(lambda: to_relaxed(t).wait_send())
        pl.when(passes_on)(lambda: passed_on(t).wait_send())

    over(0, tiles, sent)
    over(1, n, lambda d: share(d).wait_send())
    for d in range(1, slabs):
        tell(d).wait_send()
    out_rest.wait()
    over(0, tiles, lambda t: out_result(t).wait())


def per_device(n, slabs, q_start, guess):
    comp, rows, ny, nz = q_start.shape
    tiles = ny // TILE
    wide = rows + 2 * REACH
    vmem = lambda *shape: pltpu.VMEM(shape, jnp.float32)
    sems = lambda *shape: pltpu.SemaphoreType.DMA(shape)
    padded = (wide, ny + 2 * TILE, nz)
    block = (comp, rows, ny, nz)
    return pl.pallas_call(
        functools.partial(kernel, n, slabs),
        out_shape=(jax.ShapeDtypeStruct(guess.shape, jnp.float32),) * 2,
        in_specs=[pl.BlockSpec(memory_space=pl.ANY)] * 2,
        out_specs=(pl.BlockSpec(memory_space=pl.ANY),) * 2,
        scratch_shapes=[
            vmem(comp, *padded), vmem(comp, *padded), vmem(comp, *padded), vmem(comp, *padded),
            vmem(comp, *padded), vmem(comp, *padded), vmem(*padded),
            vmem(*block), vmem(*block), vmem(*block), vmem(*block), vmem(*block), vmem(*block),
            vmem(n, TILE, nz), vmem(slabs, TILE, nz),
            sems(3), sems(2, tiles), sems(2, tiles), sems(2, tiles), sems(2, tiles),
            sems(tiles), sems(tiles), sems(tiles), sems(tiles), sems(tiles),
            sems(n), sems(n), sems(slabs), sems(slabs), sems(1), sems(tiles),
        ],
        compiler_params=pltpu.CompilerParams(
            collective_id=0, has_side_effects=True, vmem_limit_bytes=60 * 1024 * 1024
        ),
    )(q_start, guess)


def solution(mesh):
    return jax.shard_map(
        functools.partial(per_device, mesh.shape["space"], mesh.shape["tm"]),
        mesh=mesh,
        in_specs=(P(None, "space", None, None), P("tm", None, "space", None, None)),
        out_specs=(P("tm", None, "space", None, None), P("tm", None, "space", None, None)),
        check_vma=False,
    )
```

```python
import functools

import jax
import jax.numpy as jnp
from jax import lax
from jax.experimental import pallas as pl
from jax.experimental.pallas import tpu as pltpu
from jax.sharding import PartitionSpec as P

STEPS_SLAB = 2
SWEEPS = 2
BLK = 4

time_step = 0.1
cross = 8.0
axial = 2.0
linear_rate = 0.1
quadratic_rate = 0.5
cubic_rate = 1.0

REACH = STEPS_SLAB * SWEEPS
TILE = 8
MESH = pl.DeviceIdType.MESH


def bulk(field):
    a, b, c, d, e = field
    f = -a - d
    aa, bb, cc, dd, ee, ff = a * a, b * b, c * c, d * d, e * e, f * f
    trace = aa + dd + ff + 2.0 * (bb + cc + ee)
    third = trace * (1.0 / 3.0)
    quad = (
        aa + bb + cc - third,
        a * b + b * d + c * e,
        a * c + b * e + c * f,
        bb + dd + ee - third,
        b * c + d * e + e * f,
    )
    source = [q + (time_step * quadratic_rate) * s for q, s in zip(field, quad)]
    constant = 1.0 + time_step * linear_rate + 2.0 * (2.0 * cross + axial)
    diagonal = constant + (time_step * cubic_rate) * trace
    return source, diagonal


def neighbours(ref, c, r, t, before, now, after):
    along_x = before + after
    along_y = ref[c, r, pl.ds(TILE * t + TILE - 1, TILE), :] + ref[c, r, pl.ds(TILE * t + TILE + 1, TILE), :]
    lanes = now.shape[1]
    along_z = pltpu.roll(now, 1, 1) + pltpu.roll(now, lanes - 1, 1)
    return (cross / axial) * (along_x + along_y) + along_z


def padded_at(t):
    return pl.ds(pl.multiple_of(TILE * t + TILE, TILE), TILE)


def tile_rows(ref, r, t):
    return [ref[c, r, padded_at(t), :] for c in range(ref.shape[0])]


def first_sweep(ref, out, src, inv, rows, inside, t):
    at = padded_at(t)
    before, now = tile_rows(ref, rows[0] - 1, t), tile_rows(ref, rows[0], t)
    for r in rows:
        after = tile_rows(ref, r + 1, t)
        source, diagonal = bulk(now)
        inverse = inside(r) / diagonal
        scaled = axial * inverse
        inv[r, at, :] = scaled
        for c in range(ref.shape[0]):
            part = source[c] * inverse
            src[c, r, at, :] = part
            out[c, r, at, :] = part + scaled * neighbours(ref, c, r, t, before[c], now[c], after[c])
        before, now = now, after


def next_sweep(ref, store, src, inv, rows, t):
    at = padded_at(t)
    before, now = tile_rows(ref, rows[0] - 1, t), tile_rows(ref, rows[0], t)
    for r in rows:
        after = tile_rows(ref, r + 1, t)
        scaled = inv[r, at, :]
        for c in range(ref.shape[0]):
            store(c, r, t, src[c, r, at, :] + scaled * neighbours(ref, c, r, t, before[c], now[c], after[c]))
        before, now = now, after


def phi(ref, store, w1, w2, w3, src, inv, inside, rows, tiles, arrive, finish, carry):
    wide = rows + 2 * REACH

    def keep(c, r, t, value):
        w2[c, r, padded_at(t), :] = value

    sweeps = (
        lambda t: first_sweep(ref, w1, src, inv, range(1, wide - 1), inside, t),
        lambda t: next_sweep(w1, keep, src, inv, range(2, wide - 2), t),
        lambda t: first_sweep(w2, w3, src, inv, range(3, wide - 3), inside, t),
        lambda t: next_sweep(w3, store, src, inv, range(4, wide - 4), t),
    )

    def turn(i, carry):
        pl.when(i < tiles)(lambda: arrive(i))
        for lag, sweep in enumerate(sweeps):
            here = jnp.logical_and(i >= lag + 1, i < tiles + lag + 1)
            pl.when(here)(functools.partial(sweep, i - lag - 1))
        low = jnp.where(i < REACH, 0, i - REACH)
        high = jnp.where(i < REACH, 0, i - REACH + 1)
        return lax.fori_loop(low, high, finish, carry)

    return lax.fori_loop(0, tiles + REACH, turn, carry)


def kernel(
    n, slabs, q_ref, g_ref, corrected_ref, residual_ref,
    e1, e2, w1, w2, w3, src, inv, x, landed, relaxed, again, guess, result, rest, sums, terms,
    load_sem, h1_send, h1_recv, h2_send, h2_recv, x_send, r_send, f_send, s_recv, r_recv,
    sum_send, sum_recv, term_send, term_recv, rest_sem, out_sem,
):
    p = lax.axis_index("tm")
    s = lax.axis_index("space")
    comp, rows, ny, nz = guess.shape
    tiles = ny // TILE
    mid = pl.ds(REACH, rows)
    body = pl.ds(TILE, ny)
    has_left, has_right = s > 0, s < n - 1

    barrier = pltpu.get_barrier_semaphore()

    def greet_space(d, carry):
        pl.semaphore_signal(barrier, inc=1, device_id={"space": lax.rem(s + d, n)}, device_id_type=MESH)
        return carry

    lax.fori_loop(1, n, greet_space, 0)
    for d in range(1, slabs):
        pl.semaphore_signal(barrier, inc=1, device_id={"tm": lax.rem(p + d, slabs)}, device_id_type=MESH)

    own = e1.at[:, mid, body, :]
    load_guess = pltpu.make_async_copy(g_ref.at[0], guess, load_sem.at[0])
    load_guess.start()
    own_guess = pltpu.make_async_copy(g_ref.at[0], own, load_sem.at[1])
    own_start = pltpu.make_async_copy(q_ref, own, load_sem.at[1])
    first_start = pltpu.make_async_copy(q_ref, e2.at[:, mid, body, :], load_sem.at[2])
    pl.when(p < slabs - 1)(own_guess.start)
    pl.when(p == slabs - 1)(own_start.start)
    pl.when(p == 0)(first_start.start)

    wide = rows + 2 * REACH
    border = jnp.zeros((TILE, nz), jnp.float32)

    def clear_pads(r, carry):
        for ref in (e1, e2, w1, w2, w3):
            for c in range(comp):
                ref[c, r, pl.ds(0, TILE), :] = border
                ref[c, r, pl.ds(TILE + ny, TILE), :] = border
        return carry

    lax.fori_loop(0, wide, clear_pads, 0)

    def clear_rows(first):
        def one(t, carry):
            at = pl.ds(pl.multiple_of(TILE * t + TILE, TILE), TILE)
            for ref in (e1, e2):
                for c in range(comp):
                    for r in range(REACH):
                        ref[c, first + r, at, :] = border
            return carry

        lax.fori_loop(0, tiles, one, 0)

    pl.when(s == 0)(functools.partial(clear_rows, 0))
    pl.when(s == n - 1)(functools.partial(clear_rows, REACH + rows))

    left_inside = jnp.where(has_left, 1.0, 0.0).astype(jnp.float32)
    right_inside = jnp.where(has_right, 1.0, 0.0).astype(jnp.float32)

    def inside(r):
        if r < REACH:
            return left_inside
        if r >= REACH + rows:
            return right_inside
        return 1.0

    pl.semaphore_wait(barrier, n - 1 + slabs - 1)

    def halo(ref, send, recv, t):
        at = pl.ds(pl.multiple_of(TILE * t + TILE, TILE), TILE)
        source = ref.at[:, mid, at, :]
        to_left = pltpu.make_async_remote_copy(
            source, ref.at[:, pl.ds(REACH + rows, REACH), at, :], send.at[0, t], recv.at[0, t],
            device_id={"space": lax.rem(s + n - 1, n)}, device_id_type=MESH,
        )
        to_right = pltpu.make_async_remote_copy(
            source, ref.at[:, pl.ds(0, REACH), at, :], send.at[1, t], recv.at[1, t],
            device_id={"space": lax.rem(s + 1, n)}, device_id_type=MESH,
        )
        return to_left, to_right

    def halo_start(ref, send, recv, t):
        to_left, to_right = halo(ref, send, recv, t)
        pl.when(has_left)(to_left.start)
        pl.when(has_right)(to_right.start)

    def halo_arrived(ref, send, recv, t):
        to_left, to_right = halo(ref, send, recv, t)
        pl.when(has_right)(to_left.wait_recv)
        pl.when(has_left)(to_right.wait_recv)

    def halo_sent(ref, send, recv, t):
        to_left, to_right = halo(ref, send, recv, t)
        pl.when(has_left)(to_left.wait_send)
        pl.when(has_right)(to_right.wait_send)

    def over(lo, hi, act):
        def one(t, carry):
            act(t)
            return carry

        lax.fori_loop(lo, hi, one, 0)

    def to_second(t):
        return pltpu.make_async_remote_copy(
            x.at[t], landed.at[t], x_send.at[t], s_recv.at[t],
            device_id={"tm": lax.rem(p + 2, slabs)}, device_id_type=MESH,
        )

    def to_relaxed(t):
        return pltpu.make_async_remote_copy(
            x.at[t], relaxed.at[t], r_send.at[t], r_recv.at[t],
            device_id={"tm": lax.rem(p + 1, slabs)}, device_id_type=MESH,
        )

    def passed_on(t):
        return pltpu.make_async_remote_copy(
            landed.at[t], relaxed.at[t], f_send.at[t], r_recv.at[t],
            device_id={"tm": lax.rem(p + slabs - 1, slabs)}, device_id_type=MESH,
        )

    sends_second = p != 2
    sends_relaxed = lax.rem(p, 2) == 0
    passes_on = p == slabs - 1

    pl.when(p < slabs - 1)(own_guess.wait)
    pl.when(p == slabs - 1)(own_start.wait)
    over(0, tiles, functools.partial(halo_start, e1, h1_send, h1_recv))

    def send(t, carry):
        pl.when(sends_second)(lambda: to_second(t).start())
        pl.when(sends_relaxed)(lambda: to_relaxed(t).start())
        return carry

    def to_x(c, r, t, value):
        x[t, c, r - REACH] = value

    def to_again(c, r, t, value):
        again[c, r - REACH, pl.ds(pl.multiple_of(TILE * t, TILE), TILE), :] = value

    phi(
        e1, to_x, w1, w2, w3, src, inv, inside, rows, tiles,
        functools.partial(halo_arrived, e1, h1_send, h1_recv), send, 0,
    )

    pl.when(p == 0)(first_start.wait)

    def take(t):
        @pl.when(p > 0)
        def _():
            to_second(t).wait_recv()
            e2[:, REACH : REACH + rows, padded_at(t), :] = landed[t]

        halo_start(e2, h2_send, h2_recv, t)
        pl.when(passes_on)(lambda: passed_on(t).start())

    def arrive(t):
        pl.when(t < tiles - 1)(lambda: take(t + 1))
        halo_arrived(e2, h2_send, h2_recv, t)

    def gather(t, totals):
        at = pl.ds(pl.multiple_of(TILE * t, TILE), TILE)
        return tuple(
            total + sum(again[c, r, at, :] - guess[c, r, at, :] for r in range(rows))
            for c, total in enumerate(totals)
        )

    load_guess.wait()
    take(0)
    totals = phi(
        e2, to_again, w1, w2, w3, src, inv, inside, rows, tiles,
        arrive, gather, tuple(border for _ in range(comp)),
    )
    sums[s] = border
    for c in range(comp):
        sums[s, pl.ds(c, 1), :] = jnp.sum(totals[c], axis=0, keepdims=True)

    def share(d):
        return pltpu.make_async_remote_copy(
            sums.at[s], sums.at[s], sum_send.at[d], sum_recv.at[s],
            device_id={"space": lax.rem(s + d, n)}, device_id_type=MESH,
        )

    def shared_arrived(d):
        source = lax.rem(s + d, n)
        pltpu.make_async_remote_copy(
            sums.at[source], sums.at[source], sum_send.at[d], sum_recv.at[source],
            device_id={"space": source}, device_id_type=MESH,
        ).wait_recv()

    over(1, n, lambda d: share(d).start())
    pl.when(p > 0)(lambda: over(0, tiles, lambda t: to_relaxed(t).wait_recv()))

    @pl.when(p == 0)
    def _():
        def same(t):
            at = pl.ds(pl.multiple_of(TILE * t, TILE), TILE)
            relaxed[t] = again[:, :, at, :]

        over(0, tiles, same)

    def subtract(t):
        at = pl.ds(pl.multiple_of(TILE * t, TILE), TILE)
        rest[:, :, at, :] = again[:, :, at, :] - relaxed[t]

    over(0, tiles, subtract)
    out_rest = pltpu.make_async_copy(rest, residual_ref.at[0], rest_sem.at[0])
    out_rest.start()
    over(1, n, shared_arrived)
    total = lax.fori_loop(0, n, lambda i, held: held + sums[i], border)

    lane = lax.broadcasted_iota(jnp.int32, (TILE, nz), 1)
    width = 1
    while width < BLK:
        upper = pltpu.roll(total, nz - width, 1)
        lower = pltpu.roll(total, width, 1)
        total = total + jnp.where((lane // width) % 2 == 0, upper, lower)
        width *= 2
    terms[p] = total * (1.0 / (rows * n * ny * BLK))

    def tell(d):
        return pltpu.make_async_remote_copy(
            terms.at[p], terms.at[p], term_send.at[d], term_recv.at[p],
            device_id={"tm": lax.rem(p + d, slabs)}, device_id_type=MESH,
        )

    for d in range(1, slabs):
        tell(d).start()
    for d in range(1, slabs):
        source = lax.rem(p + d, slabs)
        pltpu.make_async_remote_copy(
            terms.at[source], terms.at[source], term_send.at[d], term_recv.at[source],
            device_id={"tm": source}, device_id_type=MESH,
        ).wait_recv()

    decay = 1.0 / (1.0 + STEPS_SLAB * time_step * linear_rate)
    error = terms[0]
    for j in range(1, slabs):
        error = jnp.where(p >= j, decay * error + terms[j], error)
    spread = [jnp.broadcast_to(error[c : c + 1], (TILE, nz)) for c in range(comp)]

    def out_result(t):
        at = pl.ds(pl.multiple_of(TILE * t, TILE), TILE)
        return pltpu.make_async_copy(result.at[:, :, at, :], corrected_ref.at[0, :, :, at, :], out_sem.at[t])

    def correct(t):
        at = pl.ds(pl.multiple_of(TILE * t, TILE), TILE)
        for c in range(comp):
            for r in range(rows):
                result[c, r, at, :] = relaxed[t, c, r] + spread[c]
        out_result(t).start()

    over(0, tiles, correct)

    def sent(t):
        halo_sent(e1, h1_send, h1_recv, t)
        halo_sent(e2, h2_send, h2_recv, t)
        pl.when(sends_second)(lambda: to_second(t).wait_send())
        pl.when(sends_relaxed)(lambda: to_relaxed(t).wait_send())
        pl.when(passes_on)(lambda: passed_on(t).wait_send())

    over(0, tiles, sent)
    over(1, n, lambda d: share(d).wait_send())
    for d in range(1, slabs):
        tell(d).wait_send()
    out_rest.wait()
    over(0, tiles, lambda t: out_result(t).wait())


def per_device(n, slabs, q_start, guess):
    comp, rows, ny, nz = q_start.shape
    tiles = ny // TILE
    wide = rows + 2 * REACH
    vmem = lambda *shape: pltpu.VMEM(shape, jnp.float32)
    sems = lambda *shape: pltpu.SemaphoreType.DMA(shape)
    padded = (wide, ny + 2 * TILE, nz)
    block = (comp, rows, ny, nz)
    tiled = (tiles, comp, rows, TILE, nz)
    return pl.pallas_call(
        functools.partial(kernel, n, slabs),
        out_shape=(jax.ShapeDtypeStruct(guess.shape, jnp.float32),) * 2,
        in_specs=[pl.BlockSpec(memory_space=pltpu.HBM)] * 2,
        out_specs=(pl.BlockSpec(memory_space=pl.ANY),) * 2,
        scratch_shapes=[
            vmem(comp, *padded), vmem(comp, *padded), vmem(comp, *padded), vmem(comp, *padded),
            vmem(comp, *padded), vmem(comp, *padded), vmem(*padded),
            vmem(*tiled), vmem(*tiled), vmem(*tiled), vmem(*block), vmem(*block), vmem(*block), vmem(*block),
            vmem(n, TILE, nz), vmem(slabs, TILE, nz),
            sems(3), sems(2, tiles), sems(2, tiles), sems(2, tiles), sems(2, tiles),
            sems(tiles), sems(tiles), sems(tiles), sems(tiles), sems(tiles),
            sems(n), sems(n), sems(slabs), sems(slabs), sems(1), sems(tiles),
        ],
        compiler_params=pltpu.CompilerParams(
            collective_id=0, has_side_effects=True, vmem_limit_bytes=32 * 1024 * 1024
        ),
    )(q_start, guess)


def solution(mesh):
    return jax.shard_map(
        functools.partial(per_device, mesh.shape["space"], mesh.shape["tm"]),
        mesh=mesh,
        in_specs=(P(None, "space", None, None), P("tm", None, "space", None, None)),
        out_specs=(P("tm", None, "space", None, None), P("tm", None, "space", None, None)),
        check_vma=False,
    )
```

```python
import functools

import jax
import jax.numpy as jnp
from jax import lax
from jax.experimental import pallas as pl
from jax.experimental.pallas import tpu as pltpu
from jax.sharding import PartitionSpec as P

STEPS_SLAB = 2
SWEEPS = 2
BLK = 4

time_step = 0.1
cross = 8.0
axial = 2.0
linear_rate = 0.1
quadratic_rate = 0.5
cubic_rate = 1.0

REACH = STEPS_SLAB * SWEEPS
TILE = 8
AHEAD = 4
MESH = pl.DeviceIdType.MESH


def bulk(field):
    a, b, c, d, e = field
    f = -a - d
    aa, bb, cc, dd, ee, ff = a * a, b * b, c * c, d * d, e * e, f * f
    trace = aa + dd + ff + 2.0 * (bb + cc + ee)
    third = trace * (1.0 / 3.0)
    quad = (
        aa + bb + cc - third,
        a * b + b * d + c * e,
        a * c + b * e + c * f,
        bb + dd + ee - third,
        b * c + d * e + e * f,
    )
    source = [q + (time_step * quadratic_rate) * s for q, s in zip(field, quad)]
    constant = 1.0 + time_step * linear_rate + 2.0 * (2.0 * cross + axial)
    diagonal = constant + (time_step * cubic_rate) * trace
    return source, diagonal


def neighbours(ref, c, r, t, before, now, after):
    along_x = before + after
    along_y = ref[c, r, pl.ds(TILE * t + TILE - 1, TILE), :] + ref[c, r, pl.ds(TILE * t + TILE + 1, TILE), :]
    lanes = now.shape[1]
    along_z = pltpu.roll(now, 1, 1) + pltpu.roll(now, lanes - 1, 1)
    return (cross / axial) * (along_x + along_y) + along_z


def padded_at(t):
    return pl.ds(pl.multiple_of(TILE * t + TILE, TILE), TILE)


def tile_rows(ref, r, t):
    return [ref[c, r, padded_at(t), :] for c in range(ref.shape[0])]


def first_sweep(ref, out, src, inv, rows, inside, t):
    at = padded_at(t)
    before, now = tile_rows(ref, rows[0] - 1, t), tile_rows(ref, rows[0], t)
    for r in rows:
        after = tile_rows(ref, r + 1, t)
        source, diagonal = bulk(now)
        inverse = inside(r) / diagonal
        scaled = axial * inverse
        inv[r, at, :] = scaled
        for c in range(ref.shape[0]):
            part = source[c] * inverse
            src[c, r, at, :] = part
            out[c, r, at, :] = part + scaled * neighbours(ref, c, r, t, before[c], now[c], after[c])
        before, now = now, after


def next_sweep(ref, store, src, inv, rows, t):
    at = padded_at(t)
    before, now = tile_rows(ref, rows[0] - 1, t), tile_rows(ref, rows[0], t)
    for r in rows:
        after = tile_rows(ref, r + 1, t)
        scaled = inv[r, at, :]
        for c in range(ref.shape[0]):
            store(c, r, t, src[c, r, at, :] + scaled * neighbours(ref, c, r, t, before[c], now[c], after[c]))
        before, now = now, after


def phi(ref, store, w1, w2, w3, src, inv, inside, rows, tiles, arrive, finish, carry):
    wide = rows + 2 * REACH

    def keep(c, r, t, value):
        w2[c, r, padded_at(t), :] = value

    sweeps = (
        lambda t: first_sweep(ref, w1, src, inv, range(1, wide - 1), inside, t),
        lambda t: next_sweep(w1, keep, src, inv, range(2, wide - 2), t),
        lambda t: first_sweep(w2, w3, src, inv, range(3, wide - 3), inside, t),
        lambda t: next_sweep(w3, store, src, inv, range(4, wide - 4), t),
    )

    def turn(i, carry):
        pl.when(i < tiles)(lambda: arrive(i))
        for lag, sweep in enumerate(sweeps):
            here = jnp.logical_and(i >= lag + 1, i < tiles + lag + 1)
            pl.when(here)(functools.partial(sweep, i - lag - 1))
        low = jnp.where(i < REACH, 0, i - REACH)
        high = jnp.where(i < REACH, 0, i - REACH + 1)
        return lax.fori_loop(low, high, finish, carry)

    return lax.fori_loop(0, tiles + REACH, turn, carry)


def kernel(
    n, slabs, q_ref, g_ref, corrected_ref, residual_ref,
    e1, e2, w1, w2, w3, src, inv, x, landed, relaxed, again, guess, result, rest, sums, terms,
    load_sem, h1_send, h1_recv, h2_send, h2_recv, x_send, r_send, f_send, s_recv, r_recv,
    sum_send, sum_recv, term_send, term_recv, rest_sem, out_sem,
):
    p = lax.axis_index("tm")
    s = lax.axis_index("space")
    comp, rows, ny, nz = guess.shape
    tiles = ny // TILE
    mid = pl.ds(REACH, rows)
    body = pl.ds(TILE, ny)
    has_left, has_right = s > 0, s < n - 1

    barrier = pltpu.get_barrier_semaphore()

    def greet_space(d, carry):
        pl.semaphore_signal(barrier, inc=1, device_id={"space": lax.rem(s + d, n)}, device_id_type=MESH)
        return carry

    lax.fori_loop(1, n, greet_space, 0)
    for d in range(1, slabs):
        pl.semaphore_signal(barrier, inc=1, device_id={"tm": lax.rem(p + d, slabs)}, device_id_type=MESH)

    own = e1.at[:, mid, body, :]
    load_guess = pltpu.make_async_copy(g_ref.at[0], guess, load_sem.at[0])
    load_guess.start()
    own_guess = pltpu.make_async_copy(g_ref.at[0], own, load_sem.at[1])
    own_start = pltpu.make_async_copy(q_ref, own, load_sem.at[1])
    first_start = pltpu.make_async_copy(q_ref, e2.at[:, mid, body, :], load_sem.at[2])
    pl.when(p < slabs - 1)(own_guess.start)
    pl.when(p == slabs - 1)(own_start.start)
    pl.when(p == 0)(first_start.start)

    wide = rows + 2 * REACH
    border = jnp.zeros((TILE, nz), jnp.float32)

    def clear_pads(r, carry):
        for ref in (e1, e2, w1, w2, w3):
            for c in range(comp):
                ref[c, r, pl.ds(0, TILE), :] = border
                ref[c, r, pl.ds(TILE + ny, TILE), :] = border
        return carry

    lax.fori_loop(0, wide, clear_pads, 0)

    def clear_rows(first):
        def one(t, carry):
            at = pl.ds(pl.multiple_of(TILE * t + TILE, TILE), TILE)
            for ref in (e1, e2):
                for c in range(comp):
                    for r in range(REACH):
                        ref[c, first + r, at, :] = border
            return carry

        lax.fori_loop(0, tiles, one, 0)

    pl.when(s == 0)(functools.partial(clear_rows, 0))
    pl.when(s == n - 1)(functools.partial(clear_rows, REACH + rows))

    left_inside = jnp.where(has_left, 1.0, 0.0).astype(jnp.float32)
    right_inside = jnp.where(has_right, 1.0, 0.0).astype(jnp.float32)

    def inside(r):
        if r < REACH:
            return left_inside
        if r >= REACH + rows:
            return right_inside
        return 1.0

    pl.semaphore_wait(barrier, n - 1 + slabs - 1)

    def halo(ref, send, recv, t):
        at = pl.ds(pl.multiple_of(TILE * t + TILE, TILE), TILE)
        source = ref.at[:, mid, at, :]
        to_left = pltpu.make_async_remote_copy(
            source, ref.at[:, pl.ds(REACH + rows, REACH), at, :], send.at[0, t], recv.at[0, t],
            device_id={"space": lax.rem(s + n - 1, n)}, device_id_type=MESH,
        )
        to_right = pltpu.make_async_remote_copy(
            source, ref.at[:, pl.ds(0, REACH), at, :], send.at[1, t], recv.at[1, t],
            device_id={"space": lax.rem(s + 1, n)}, device_id_type=MESH,
        )
        return to_left, to_right

    def halo_start(ref, send, recv, t):
        to_left, to_right = halo(ref, send, recv, t)
        pl.when(has_left)(to_left.start)
        pl.when(has_right)(to_right.start)

    def halo_arrived(ref, send, recv, t):
        to_left, to_right = halo(ref, send, recv, t)
        pl.when(has_right)(to_left.wait_recv)
        pl.when(has_left)(to_right.wait_recv)

    def halo_sent(ref, send, recv, t):
        to_left, to_right = halo(ref, send, recv, t)
        pl.when(has_left)(to_left.wait_send)
        pl.when(has_right)(to_right.wait_send)

    def over(lo, hi, act):
        def one(t, carry):
            act(t)
            return carry

        lax.fori_loop(lo, hi, one, 0)

    def to_second(t):
        return pltpu.make_async_remote_copy(
            x.at[t], landed.at[t], x_send.at[t], s_recv.at[t],
            device_id={"tm": lax.rem(p + 2, slabs)}, device_id_type=MESH,
        )

    def to_relaxed(t):
        return pltpu.make_async_remote_copy(
            x.at[t], relaxed.at[t], r_send.at[t], r_recv.at[t],
            device_id={"tm": lax.rem(p + 1, slabs)}, device_id_type=MESH,
        )

    def passed_on(t):
        return pltpu.make_async_remote_copy(
            landed.at[t], relaxed.at[t], f_send.at[t], r_recv.at[t],
            device_id={"tm": lax.rem(p + slabs - 1, slabs)}, device_id_type=MESH,
        )

    sends_second = p != 2
    sends_relaxed = lax.rem(p, 2) == 0
    passes_on = p == slabs - 1

    pl.when(p < slabs - 1)(own_guess.wait)
    pl.when(p == slabs - 1)(own_start.wait)
    over(0, tiles, functools.partial(halo_start, e1, h1_send, h1_recv))

    pl.when(p == 0)(first_start.wait)

    def take(t):
        @pl.when(p > 0)
        def _():
            to_second(t).wait_recv()
            e2[:, REACH : REACH + rows, padded_at(t), :] = landed[t]

        halo_start(e2, h2_send, h2_recv, t)
        pl.when(passes_on)(lambda: passed_on(t).start())

    def send(t, carry):
        pl.when(sends_second)(lambda: to_second(t).start())
        pl.when(sends_relaxed)(lambda: to_relaxed(t).start())
        pl.when(t >= AHEAD)(lambda: take(t - AHEAD))
        return carry

    def to_x(c, r, t, value):
        x[t, c, r - REACH] = value

    def to_again(c, r, t, value):
        again[c, r - REACH, pl.ds(pl.multiple_of(TILE * t, TILE), TILE), :] = value

    phi(
        e1, to_x, w1, w2, w3, src, inv, inside, rows, tiles,
        functools.partial(halo_arrived, e1, h1_send, h1_recv), send, 0,
    )

    def arrive(t):
        pl.when(jnp.logical_and(t >= tiles - AHEAD - 1, t < tiles - 1))(lambda: take(t + 1))
        halo_arrived(e2, h2_send, h2_recv, t)

    def gather(t, totals):
        at = pl.ds(pl.multiple_of(TILE * t, TILE), TILE)
        return tuple(
            total + sum(again[c, r, at, :] - guess[c, r, at, :] for r in range(rows))
            for c, total in enumerate(totals)
        )

    load_guess.wait()
    totals = phi(
        e2, to_again, w1, w2, w3, src, inv, inside, rows, tiles,
        arrive, gather, tuple(border for _ in range(comp)),
    )
    sums[s] = border
    for c in range(comp):
        sums[s, pl.ds(c, 1), :] = jnp.sum(totals[c], axis=0, keepdims=True)

    def share(d):
        return pltpu.make_async_remote_copy(
            sums.at[s], sums.at[s], sum_send.at[d], sum_recv.at[s],
            device_id={"space": lax.rem(s + d, n)}, device_id_type=MESH,
        )

    def shared_arrived(d):
        source = lax.rem(s + d, n)
        pltpu.make_async_remote_copy(
            sums.at[source], sums.at[source], sum_send.at[d], sum_recv.at[source],
            device_id={"space": source}, device_id_type=MESH,
        ).wait_recv()

    over(1, n, lambda d: share(d).start())
    pl.when(p > 0)(lambda: over(0, tiles, lambda t: to_relaxed(t).wait_recv()))

    @pl.when(p == 0)
    def _():
        def same(t):
            at = pl.ds(pl.multiple_of(TILE * t, TILE), TILE)
            relaxed[t] = again[:, :, at, :]

        over(0, tiles, same)

    def subtract(t):
        at = pl.ds(pl.multiple_of(TILE * t, TILE), TILE)
        rest[:, :, at, :] = again[:, :, at, :] - relaxed[t]

    over(0, tiles, subtract)
    out_rest = pltpu.make_async_copy(rest, residual_ref.at[0], rest_sem.at[0])
    out_rest.start()
    over(1, n, shared_arrived)
    total = lax.fori_loop(0, n, lambda i, held: held + sums[i], border)

    lane = lax.broadcasted_iota(jnp.int32, (TILE, nz), 1)
    width = 1
    while width < BLK:
        upper = pltpu.roll(total, nz - width, 1)
        lower = pltpu.roll(total, width, 1)
        total = total + jnp.where((lane // width) % 2 == 0, upper, lower)
        width *= 2
    terms[p] = total * (1.0 / (rows * n * ny * BLK))

    def tell(d):
        return pltpu.make_async_remote_copy(
            terms.at[p], terms.at[p], term_send.at[d], term_recv.at[p],
            device_id={"tm": lax.rem(p + d, slabs)}, device_id_type=MESH,
        )

    for d in range(1, slabs):
        tell(d).start()
    for d in range(1, slabs):
        source = lax.rem(p + d, slabs)
        pltpu.make_async_remote_copy(
            terms.at[source], terms.at[source], term_send.at[d], term_recv.at[source],
            device_id={"tm": source}, device_id_type=MESH,
        ).wait_recv()

    decay = 1.0 / (1.0 + STEPS_SLAB * time_step * linear_rate)
    error = terms[0]
    for j in range(1, slabs):
        error = jnp.where(p >= j, decay * error + terms[j], error)
    spread = [jnp.broadcast_to(error[c : c + 1], (TILE, nz)) for c in range(comp)]

    def out_result(t):
        at = pl.ds(pl.multiple_of(TILE * t, TILE), TILE)
        return pltpu.make_async_copy(result.at[:, :, at, :], corrected_ref.at[0, :, :, at, :], out_sem.at[t])

    def correct(t):
        at = pl.ds(pl.multiple_of(TILE * t, TILE), TILE)
        for c in range(comp):
            for r in range(rows):
                result[c, r, at, :] = relaxed[t, c, r] + spread[c]
        out_result(t).start()

    over(0, tiles, correct)

    def sent(t):
        halo_sent(e1, h1_send, h1_recv, t)
        halo_sent(e2, h2_send, h2_recv, t)
        pl.when(sends_second)(lambda: to_second(t).wait_send())
        pl.when(sends_relaxed)(lambda: to_relaxed(t).wait_send())
        pl.when(passes_on)(lambda: passed_on(t).wait_send())

    over(0, tiles, sent)
    over(1, n, lambda d: share(d).wait_send())
    for d in range(1, slabs):
        tell(d).wait_send()
    out_rest.wait()
    over(0, tiles, lambda t: out_result(t).wait())


def per_device(n, slabs, q_start, guess):
    comp, rows, ny, nz = q_start.shape
    tiles = ny // TILE
    wide = rows + 2 * REACH
    vmem = lambda *shape: pltpu.VMEM(shape, jnp.float32)
    sems = lambda *shape: pltpu.SemaphoreType.DMA(shape)
    padded = (wide, ny + 2 * TILE, nz)
    block = (comp, rows, ny, nz)
    tiled = (tiles, comp, rows, TILE, nz)
    return pl.pallas_call(
        functools.partial(kernel, n, slabs),
        out_shape=(jax.ShapeDtypeStruct(guess.shape, jnp.float32),) * 2,
        in_specs=[pl.BlockSpec(memory_space=pltpu.HBM)] * 2,
        out_specs=(pl.BlockSpec(memory_space=pl.ANY),) * 2,
        scratch_shapes=[
            vmem(comp, *padded), vmem(comp, *padded), vmem(comp, *padded), vmem(comp, *padded),
            vmem(comp, *padded), vmem(comp, *padded), vmem(*padded),
            vmem(*tiled), vmem(*tiled), vmem(*tiled), vmem(*block), vmem(*block), vmem(*block), vmem(*block),
            vmem(n, TILE, nz), vmem(slabs, TILE, nz),
            sems(3), sems(2, tiles), sems(2, tiles), sems(2, tiles), sems(2, tiles),
            sems(tiles), sems(tiles), sems(tiles), sems(tiles), sems(tiles),
            sems(n), sems(n), sems(slabs), sems(slabs), sems(1), sems(tiles),
        ],
        compiler_params=pltpu.CompilerParams(
            collective_id=0, has_side_effects=True, vmem_limit_bytes=53 * 1024 * 1024
        ),
    )(q_start, guess)


def solution(mesh):
    return jax.shard_map(
        functools.partial(per_device, mesh.shape["space"], mesh.shape["tm"]),
        mesh=mesh,
        in_specs=(P(None, "space", None, None), P("tm", None, "space", None, None)),
        out_specs=(P("tm", None, "space", None, None), P("tm", None, "space", None, None)),
        check_vma=False,
    )
```
